256 devices in a mesh: section: 8 (over z_hi, core), attn: 32 (over y, z_lo, x).
Axes of the slice: x: 4, y: 4, z: 8 (z_hi: 4, z_lo: 2; z = z_hi * 2 + z_lo), core: 2. Of those that a mesh axis runs over, the one named last changes fastest.
Arguments:
- queries: bfloat16 [8, 4096, 4096], P('section', 'attn'), may hold values from -150 to 150
- keys: bfloat16 [8, 4096, 512], P('section', 'attn'), may hold values from -6 to 6
- values: bfloat16 [8, 4096, 512], P('section', 'attn'), may hold values from -6 to 6
- handoff: bfloat16 [8, 4096, 8192], P('section', 'attn'), may hold values from -6 to 6
- doc_lengths: int32 [8, 8], P('section'), may hold values from 1 to 1024, 4096 in all within a row
- task_lengths: int32 [8, 32, 32], P('section'), may hold values from 1 to 8, 128 in all within a row
- assignment: int32 [8, 32, 32], P('section'), may hold values from 0 to 31, each once within a row
Outputs:
- context: bfloat16 [8, 4096, 4096], P('section', 'attn')
- task_lse: float32 [8, 8192, 32], P('section', 'attn')
- received: bfloat16 [8, 4096, 8192], P('section', 'attn')
The draws below stay inside these ranges and needn't reach their ends.
Inputs may be any that keep to these rules, and one draw needn't show every extreme that they name: `doc_lengths`: documents follow one another along each section's sequence in the order given. `task_lengths`: row [s, j] cuts owner j's 128 tokens, in order, into 32 tasks. `assignment`: row [s, j] sends owner j's 32 tasks to 32 different workers.
All inputs are finite; a program needn't handle non-finite values.
Results may differ from the reference program's by a relative error of at most 0.0046.
Values may be sent and summed in bfloat16 or wider, within the bound.
A program may use at most 128 MiB of HBM per device.

```python
import math
import jax
import jax.numpy as jnp
import numpy as np
from jax import lax

D = 8192
HQ = 32
HK = 4
HD = 128
TOK_DEV = 128
DOC_MAX = 1024
S = 4096
CAP = 8
NDOC = 8
N_SECTION = 8
N_ATTN = 32


def common_rows(key):
    shared = jax.random.normal(jax.random.fold_in(key, 101), (N_SECTION, S, HK * HD), jnp.float32)
    shared = jnp.clip(shared, -6.0, 6.0)
    return shared


def draw_keys(key, part):
    shared = common_rows(key)
    return shared.astype(jnp.bfloat16)


def draw_queries(key, part):
    key = jax.random.fold_in(key, 2)
    drawn = jnp.clip(jax.random.normal(key, (N_SECTION, S, HQ * HD), jnp.float32), -6.0, 6.0)
    return drawn.astype(jnp.bfloat16)


def levels(rng, shape, split, least, high):
    def one(axis_at, shards_of):
        heights = jax.random.uniform(jax.random.fold_in(jax.random.fold_in(rng, 6), axis_at), (shards_of,), jnp.float32, least / len(split), high / len(split))
        return jnp.repeat(jnp.exp(heights), shape[axis_at] // shards_of).reshape((-1,) + (1,) * (len(shape) - axis_at - 1))

    level = one(*split[0])
    for cut in split[1:]:
        level = level * one(*cut)
    return level


def profile(count, total, bound, lean):
    weights = [(1 << 20) // math.isqrt(standing ** lean) + 1 for standing in range(2, count + 1)]
    spare, counts = total - bound - (count - 1), [1] * (count - 1)
    while spare > 0:
        free = [i for i in range(count - 1) if counts[i] < bound]
        pool, left = sum([weights[i] for i in free]), spare
        for i in free:
            more = min(bound - counts[i], max(1, left * weights[i] // pool), spare)
            counts[i] = counts[i] + more
            spare = spare - more
    return np.array([bound] + counts)


def uneven_parts(rng, count, total, limit, skew):
    if count == 2:
        one = jax.random.randint(rng, (), max(1, total - limit), min(limit, total - 1) + 1)
        return jnp.stack([one, total - one])
    tallies = jnp.asarray(profile(count, total, limit, skew), jnp.int32)
    pairs = (count - 1) // 2
    source_of, taker = tallies[1:1 + 2 * pairs:2], tallies[2:2 + 2 * pairs:2]
    room = jnp.minimum(source_of - 1, limit - taker)
    moved = jax.random.randint(jax.random.fold_in(rng, 1), (pairs,), 0, 1 << 20) % (room + 1)
    tallies = tallies.at[1:1 + 2 * pairs:2].set(source_of - moved).at[2:2 + 2 * pairs:2].set(taker + moved)
    return tallies[jax.random.permutation(jax.random.fold_in(rng, 2), count)]


def normal_values(own_key, shape, scale, reach, cuts=(), kind=jnp.bfloat16):
    values = jax.random.normal(own_key, shape, jnp.float32) * scale
    if len(cuts) > 0:
        values = levels(own_key, shape, cuts, -0.22, 0.18) * values
    return jnp.clip(values, min=-reach, max=reach).astype(kind)


def setup_inputs(seed: int = 0) -> dict:
    streams_of = jax.random.split(jax.random.key(seed), 8)
    queries = draw_queries(jax.random.fold_in(streams_of[7], 71), 0)
    keys = draw_keys(jax.random.fold_in(streams_of[7], 71), 0)
    values = normal_values(streams_of[2], (N_SECTION, S, HK * HD), 1.0, 6.0, ((0, 8), (1, 32)))
    handoff = normal_values(streams_of[3], (N_SECTION, S, D), 1.0, 6.0, ((0, 8), (1, 32)))
    doc_lengths = jax.vmap(lambda own: uneven_parts(own, NDOC, S, DOC_MAX, 2))(jax.random.split(streams_of[4], N_SECTION)).reshape((N_SECTION, NDOC)).astype(jnp.int32)
    task_lengths = jax.vmap(lambda own: uneven_parts(own, N_ATTN, TOK_DEV, CAP, 1))(jax.random.split(streams_of[5], N_SECTION * N_ATTN)).reshape((N_SECTION, N_ATTN, N_ATTN)).astype(jnp.int32)
    assignment = jax.vmap(lambda own: jax.random.permutation(own, N_ATTN))(jax.random.split(streams_of[6], N_SECTION * N_ATTN)).reshape((N_SECTION, N_ATTN, N_ATTN)).astype(jnp.int32)
    return {"queries": queries, "keys": keys, "values": values, "handoff": handoff, "doc_lengths": doc_lengths, "task_lengths": task_lengths, "assignment": assignment}


def doc_of(positions, lengths):
    ends = jnp.cumsum(lengths).astype(jnp.int32)
    found = jnp.sum((positions[..., None] >= ends).astype(jnp.int32), -1).astype(jnp.int32)
    return jnp.where(positions < 0, -1, found).astype(jnp.int32)


def attend(query_rows, query_pos, key_window, value_window, key_pos, lengths):
    group = HQ // HK
    count = query_rows.shape[0]
    width = key_window.shape[0]
    query_heads = query_rows.astype(jnp.float32).reshape(count, HK, group, HD)
    key_heads = key_window.astype(jnp.float32).reshape(width, HK, HD)
    value_heads = value_window.astype(jnp.float32).reshape(width, HK, HD)
    scores = jnp.einsum("rhgd,khd->hgrk", query_heads, key_heads) * (HD ** -0.5)
    query_doc = doc_of(query_pos, lengths)
    key_doc = doc_of(key_pos, lengths)
    allowed = (key_doc[None, :] == query_doc[:, None]) & (key_pos[None, :] <= query_pos[:, None]) & (key_pos[None, :] >= 0)
    scores = jnp.where(allowed, scores, jnp.float32(-1e30))
    highest = jnp.max(scores, -1, keepdims=True)
    raised = jnp.exp(scores - highest)
    total = jnp.sum(raised, -1, keepdims=True)
    weights = (raised / total).astype(jnp.bfloat16).astype(jnp.float32)
    output = jnp.einsum("hgrk,khd->rhgd", weights, value_heads)
    output = output.reshape(count, HQ * HD).astype(jnp.bfloat16)
    stats = (highest[..., 0] + jnp.log(total[..., 0])).transpose(2, 0, 1).reshape(count, HQ)
    return output, stats


def one_section(queries, keys, values, doc_lengths, task_lengths, assignment):
    span = DOC_MAX + TOK_DEV
    key_pad = jnp.concatenate([jnp.zeros((DOC_MAX, HK * HD), keys.dtype), keys], 0)
    value_pad = jnp.concatenate([jnp.zeros((DOC_MAX, HK * HD), values.dtype), values], 0)

    def block(owner):
        first = (owner * TOK_DEV).astype(jnp.int32)
        query_rows = lax.dynamic_slice_in_dim(queries, first, TOK_DEV, 0)
        key_window = lax.dynamic_slice_in_dim(key_pad, first, span, 0)
        value_window = lax.dynamic_slice_in_dim(value_pad, first, span, 0)
        query_pos = (first + jnp.arange(TOK_DEV, dtype=jnp.int32)).astype(jnp.int32)
        key_pos = (first - DOC_MAX + jnp.arange(span, dtype=jnp.int32)).astype(jnp.int32)
        return attend(query_rows, query_pos, key_window, value_window, key_pos, doc_lengths)

    context, stats = lax.map(block, jnp.arange(N_ATTN, dtype=jnp.int32))
    context = context.reshape(S, HQ * HD)
    stats = stats.reshape(S, HQ)
    offsets = (jnp.cumsum(task_lengths, axis=1) - task_lengths).astype(jnp.int32)
    workers = jnp.arange(N_ATTN, dtype=jnp.int32)
    picked = assignment[:, None, :] == workers[None, :, None]
    start = jnp.sum(jnp.where(picked, offsets[:, None, :], 0), -1).astype(jnp.int32)
    start = (start + workers[:, None] * TOK_DEV).astype(jnp.int32)
    length = jnp.sum(jnp.where(picked, task_lengths[:, None, :], 0), -1).astype(jnp.int32)
    slots = jnp.arange(CAP, dtype=jnp.int32)
    index = (start.T[:, :, None] + slots[None, None, :]).astype(jnp.int32)
    filled = slots[None, None, :] < length.T[:, :, None]
    padded = jnp.concatenate([stats, jnp.zeros((CAP, HQ), stats.dtype)], 0)
    task_stats = jnp.where(filled[..., None], padded[index], jnp.float32(0.0))
    return context, task_stats.reshape(N_ATTN * N_ATTN * CAP, HQ)


def reference(queries, keys, values, handoff, doc_lengths, task_lengths, assignment):
    def per_section(pieces):
        return one_section(*pieces)

    context, task_lse = lax.map(per_section, (queries, keys, values, doc_lengths, task_lengths, assignment))
    received = jnp.concatenate([jnp.zeros_like(handoff[:1]), handoff[:-1]], 0)
    return context, task_lse, received
```

```python
import math

import jax
import jax.numpy as jnp
from jax import lax
from jax.experimental import pallas as pl
from jax.experimental.pallas import tpu as pltpu
from jax.sharding import PartitionSpec as P

MESH = pl.DeviceIdType.MESH
F32 = jnp.float32
BF16 = jnp.bfloat16
HQ = 32
HK = 4
HD = 128
GROUP = HQ // HK
ROWS = 128
WIDE = 8192
ROLES = 9
LONG = 3
PIECE = 16
SCALE = HD ** -0.5
EXP2 = SCALE / math.log(2.0)


def section_of(z, core):
    return (z // 2) * 2 + core


def owner_of(y, z, x):
    return y * 8 + (z % 2) * 4 + x


def long_pieces(z):
    return jnp.where((z == 1) | (z == 4), 3, jnp.where((z == 2) | (z == 3), 2, 0))


def kernel(
    q_hbm, k_hbm, v_hbm, h_hbm, dl_hbm, tl_hbm, as_hbm,
    ctx, lse, rec,
    qs, kb, vb, sc, mx, rl, stat, mid, ends, tl, ws,
    pack, t1, t2, t3,
    q_sem, own_sem, int_sem, kv_send, kv_recv, h_send, h_recv, m_send, m_recv,
    s_send, s_recv,
):
    s = lax.axis_index("section")
    a = lax.axis_index("attn")
    core = s % 2
    y = a // 8
    zl = (a // 4) % 2
    x = a % 4
    z = (s // 2) * 2 + zl
    up = (z + 3) % 8
    down = (z + 5) % 8
    right = a - x + (x + 1) % 4
    left = a - x + (x + 3) % 4

    sender = (core == 1) & (z < 6)
    own_long = jnp.where(core == 1, long_pieces(z), 0)
    mid_long = jnp.where(core == 0, long_pieces(up), 0)
    is_sender = own_long > 0
    is_mid = mid_long > 0
    last_long = jnp.where((core == 0) & (z >= 2), long_pieces((z + 6) % 8), 0)
    is_last = last_long > 0

    for h in range(HQ):
        pltpu.make_async_copy(
            q_hbm.at[0, :, pl.ds(h * HD, HD)], qs.at[h], q_sem.at[h]
        ).start()
    own = [
        pltpu.make_async_copy(k_hbm.at[0], kb.at[0], own_sem.at[0]),
        pltpu.make_async_copy(v_hbm.at[0], vb.at[0], own_sem.at[1]),
    ]
    ints = [
        pltpu.make_async_copy(dl_hbm, ends, int_sem.at[0]),
        pltpu.make_async_copy(tl_hbm.at[0], tl, int_sem.at[1]),
        pltpu.make_async_copy(as_hbm.at[0], ws, int_sem.at[2]),
    ]
    for copy in own + ints:
        copy.start()

    barrier = pltpu.get_barrier_semaphore()

    def greet(device):
        pl.semaphore_signal(barrier, inc=1, device_id=device, device_id_type=MESH)

    @pl.when(s > 0)
    def _():
        greet((s - 1, a))

    @pl.when(is_mid)
    def _():
        greet((section_of(up, 1), owner_of(y, up, x)))

    @pl.when(is_last)
    def _():
        greet((section_of(up, 0), owner_of(y, up, x)))

    @pl.when((zl == 1) | (y > 0))
    def _():
        greet((s, a - 4))

    @pl.when(zl == 0)
    def _():
        greet((s, a + 4))

    @pl.when((zl == 1) & (y == 0))
    def _():
        pass

    for d in range(1, 4):
        greet((s, a - x + (x + d) % 4))
        greet((s, (a + 8 * d) % 32))
    expected = 6 + jnp.where(s < 7, 1, 0) + jnp.where(is_sender, 1, 0) + jnp.where(is_mid, 1, 0)
    expected = expected + jnp.where((zl == 0) | (y < 3), 1, 0) + jnp.where(zl == 1, 1, 0)
    pl.semaphore_wait(barrier, expected)

    hbm = (k_hbm, v_hbm)
    buf = (kb, vb)

    def block(t, n, source, role, device):
        return pltpu.make_async_remote_copy(
            source, buf[t].at[role], kv_send.at[t, n], kv_recv.at[t, role],
            device_id=(s, device), device_id_type=MESH,
        )

    c_ok = (zl == 1) | (y > 0)
    odd = x % 2 == 1
    across = jnp.minimum(a + 4, 31)
    above = jnp.minimum(a + 8, 31)

    def transfers(t):
        return [
            (y < 3, block(t, 0, hbm[t].at[0], 1, above)),
            ((zl == 0) | (y < 3), block(t, 1, hbm[t].at[0], 2, across)),
            (x < 3, block(t, 2, hbm[t].at[0], 4, right)),
            (x == 0, block(t, 3, hbm[t].at[0], 3, left)),
            ((x == 3) & (y > 0), block(t, 4, buf[t].at[1], 4, right)),
            ((x > 0) & (y > 0), block(t, 5, buf[t].at[1], 3, left)),
            (c_ok, block(t, 6, buf[t].at[2], 6, right)),
            (c_ok, block(t, 7, buf[t].at[2], 5, left)),
            (odd & ((x == 3) | (y > 0)), block(t, 8, buf[t].at[3], 7, left)),
            ((x % 2 == 0) & ((x == 2) | (y > 0)), block(t, 9, buf[t].at[4], 7, right)),
            ((x % 2 == 0) & c_ok, block(t, 10, buf[t].at[5], 8, left)),
            (odd & c_ok, block(t, 11, buf[t].at[6], 8, right)),
        ]

    moves = (transfers(0), transfers(1))

    def send(t, *numbers):
        for n in numbers:
            cond, copy = moves[t][n]
            pl.when(cond)(copy.start)

    base = a - x

    def straight(other):
        return base + other - jnp.where(other > x, 8, 0)

    def crossed(other):
        return base - 4 + other

    xr, xl, xo = (x + 1) % 4, (x + 3) % 4, (x + 2) % 4
    owners = [
        a, a - 8, a - 4, straight(xr), straight(xl), crossed(xr), crossed(xl),
        straight(xo), crossed(xo),
    ]

    def arrive(t, role):
        @pl.when(owners[role] >= 0)
        def _():
            block(t, 0, hbm[t].at[0], role, a).wait_recv()

        @pl.when(owners[role] < 0)
        def _():
            buf[t][role] = jnp.zeros((ROWS, HK * HD), BF16)

    nxt = jnp.minimum(s + 1, 7)

    def direct(lo, rows, i):
        return pltpu.make_async_remote_copy(
            h_hbm.at[0, pl.ds(lo, rows)], rec.at[0, pl.ds(lo, rows)],
            h_send.at[i], h_recv.at[i], device_id=(nxt, a), device_id_type=MESH,
        )

    def piece(i):
        return direct(i * PIECE, PIECE, i)

    main = direct(LONG * PIECE, ROWS - LONG * PIECE, LONG)

    def leg1(i):
        return pltpu.make_async_remote_copy(
            h_hbm.at[0, pl.ds(i * PIECE, PIECE)], mid.at[pl.ds(i * PIECE, PIECE)],
            m_send.at[i], m_recv.at[i],
            device_id=(section_of(down, 0), owner_of(y, down, x)), device_id_type=MESH,
        )

    def leg2(i):
        return pltpu.make_async_remote_copy(
            mid.at[pl.ds(i * PIECE, PIECE)], rec.at[0, pl.ds(i * PIECE, PIECE)],
            m_send.at[LONG + i], h_recv.at[i],
            device_id=(section_of(down, 0), owner_of(y, down, x)), device_id_type=MESH,
        )

    def relay(i):
        @pl.when(mid_long > i)
        def _():
            leg1(i).wait_recv()
            leg2(i).start()

    send(0, 0, 1, 2, 3)
    send(1, 0, 1, 2, 3)
    for i in range(LONG):
        pl.when(own_long > i)(leg1(i).start)

    @pl.when(s < 7)
    def _():
        main.start()

    for i in range(LONG):
        pl.when((s < 7) & (own_long <= i))(piece(i).start)

    @pl.when(s == 0)
    def _():
        rec[...] = jnp.zeros_like(rec)

    for copy in ints + own:
        copy.wait()

    row = lax.broadcasted_iota(jnp.int32, (ROWS, ROWS), 0)
    lane = lax.broadcasted_iota(jnp.int32, (ROWS, ROWS), 1)
    position = a * ROWS + row
    first = jnp.zeros((ROWS, ROWS), jnp.int32)
    end = jnp.int32(0)
    for i in range(8):
        end = end + ends[0, i]
        first = jnp.where(position >= end, end, first)

    for h in range(HQ):
        pltpu.make_async_copy(
            q_hbm.at[0, :, pl.ds(h * HD, HD)], qs.at[h], q_sem.at[h]
        ).wait()

    def scores(role):
        key_pos = owners[role] * ROWS + lane
        bias = jnp.where((key_pos >= first) & (key_pos <= position), F32(0), F32(-1e30))

        def body(g, carry):
            keys = kb[role, :, pl.ds(pl.multiple_of(g * HD, HD), HD)]
            heads = pl.ds(g * GROUP, GROUP)
            found = lax.dot_general(
                qs[heads].reshape(GROUP * ROWS, HD), keys, (((1,), (1,)), ((), ())),
                preferred_element_type=F32,
            ).reshape(GROUP, ROWS, ROWS) + bias[None]
            sc[heads, :, role * ROWS:(role + 1) * ROWS] = found
            mx[heads] = found if role == 0 else jnp.maximum(mx[heads], found)
            return carry

        lax.fori_loop(0, HK, body, 0)

    scores(0)
    arrive(0, 1)
    send(0, 4, 5)
    arrive(0, 2)
    send(0, 6, 7)
    scores(1)
    arrive(1, 1)
    send(1, 4, 5)
    scores(2)
    arrive(1, 2)
    send(1, 6, 7)
    arrive(0, 3)
    arrive(0, 4)
    send(0, 8, 9)
    scores(3)
    scores(4)
    arrive(0, 5)
    arrive(0, 6)
    send(0, 10, 11)
    scores(5)
    scores(6)
    arrive(1, 3)
    arrive(1, 4)
    send(1, 8, 9)
    relay(0)
    arrive(1, 5)
    arrive(1, 6)
    send(1, 10, 11)
    arrive(0, 7)
    scores(7)
    arrive(0, 8)
    scores(8)
    relay(1)

    stat[...] = jnp.zeros_like(stat)

    def soft(h, carry):
        top = jnp.max(mx[h], axis=1, keepdims=True)
        raised = jnp.exp2((sc[h] - top) * F32(EXP2))
        total = jnp.sum(raised, axis=1, keepdims=True)
        sc[h] = raised
        rl[h] = jnp.broadcast_to(1.0 / total, (ROWS, ROWS))
        value = top * F32(SCALE) + jnp.log(total)
        stat[...] = jnp.where(lane == h, value, stat[...])
        return carry

    lax.fori_loop(0, HQ, soft, 0)
    relay(2)

    slots = lax.broadcasted_iota(jnp.int32, (256, 32), 0)
    tasks = lax.broadcasted_iota(jnp.int32, (256, 32), 1)
    lengths = tl[pl.ds(a, 1), :]
    workers = ws[pl.ds(a, 1), :]
    picked = workers == slots // 8
    which = jnp.sum(jnp.where(picked, tasks, 0), axis=1, keepdims=True)
    length = jnp.sum(jnp.where(picked, lengths, 0), axis=1, keepdims=True)
    start = jnp.sum(jnp.where(tasks < which, lengths, 0), axis=1, keepdims=True)
    rank = lax.broadcasted_iota(jnp.int32, (256, ROWS), 0) % 8
    token = lax.broadcasted_iota(jnp.int32, (256, ROWS), 1)
    table = jnp.where((token == start + rank) & (rank < length), F32(1), F32(0))
    packed = jnp.zeros((64, ROWS), F32)
    for i in range(4):
        moved = stat[...] if i == 0 else pltpu.roll(stat[...], 32 * i, 1)
        packed = packed + lax.dot_general(
            table[i * 64:(i + 1) * 64], moved, (((1,), (0,)), ((), ())),
            precision=lax.Precision.HIGHEST, preferred_element_type=F32,
        )
    pack[...] = packed.reshape(2, 4, 8, ROWS)

    other_z = jnp.where(zl == 0, a + 4, a - 4)
    stage1 = pltpu.make_async_remote_copy(
        pack.at[1 - zl], t1.at[zl], s_send.at[0], s_recv.at[0],
        device_id=(s, other_z), device_id_type=MESH,
    )
    stage1.start()
    t1[pl.ds(zl, 1)] = pack[pl.ds(zl, 1)]

    for role in (7, 8):
        arrive(1, role)

    def weighted(h, carry):
        weights = (sc[h] * jnp.tile(rl[h], (1, ROLES))).astype(BF16)
        lanes = pl.ds(pl.multiple_of((h // GROUP) * HD, HD), HD)
        rows = vb[:, :, lanes].reshape(ROLES * ROWS, HD)
        out = lax.dot_general(
            weights, rows, (((1,), (0,)), ((), ())), preferred_element_type=F32
        )
        ctx[0, :, pl.ds(pl.multiple_of(h * HD, HD), HD)] = out.astype(BF16)
        return carry

    lax.fori_loop(0, 8, weighted, 0)

    stage1.wait()
    stage2 = [
        pltpu.make_async_remote_copy(
            t1.at[:, (x + d) % 4], t2.at[x], s_send.at[d], s_recv.at[d],
            device_id=(s, base + (x + d) % 4), device_id_type=MESH,
        )
        for d in range(1, 4)
    ]
    for copy in stage2:
        copy.start()
    t2[pl.ds(x, 1)] = t1[:, pl.ds(x, 1)].reshape(1, 2, 8, ROWS)
    lax.fori_loop(8, 16, weighted, 0)
    for copy in stage2:
        copy.wait()
    stage3 = [
        pltpu.make_async_remote_copy(
            t2, t3.at[y], s_send.at[3 + d], s_recv.at[3 + d],
            device_id=(s, (a + 8 * d) % 32), device_id_type=MESH,
        )
        for d in range(1, 4)
    ]
    for copy in stage3:
        copy.start()
    t3[pl.ds(y, 1)] = t2[...].reshape(1, 4, 2, 8, ROWS)
    lax.fori_loop(16, HQ, weighted, 0)
    for copy in stage3:
        copy.wait()
    for from_y in range(4):
        for from_z in range(2):
            for from_x in range(4):
                tile = t3[from_y, from_x, from_z]
                mine = tile[:, 0:32]
                for i in range(1, 4):
                    mine = jnp.where(y == i, tile[:, 32 * i:32 * (i + 1)], mine)
                owner = from_y * 8 + from_z * 4 + from_x
                lse[0, owner * 8:(owner + 1) * 8, :] = mine

    for t in range(2):
        for cond, copy in moves[t]:
            pl.when(cond)(copy.wait_send)
    for i in range(LONG):
        pl.when(own_long > i)(leg1(i).wait_send)
        pl.when(mid_long > i)(leg2(i).wait_send)
        pl.when((s < 7) & (own_long <= i))(piece(i).wait_send)

    @pl.when(s < 7)
    def _():
        main.wait_send()

    @pl.when(s > 0)
    def _():
        for i in range(LONG):
            piece(i).wait_recv()
        main.wait_recv()


def shards(queries, keys, values, handoff, doc_lengths, task_lengths, assignment):
    anywhere = pl.BlockSpec(memory_space=pltpu.HBM)
    local = pl.BlockSpec(memory_space=pltpu.VMEM)
    dma = pltpu.SemaphoreType.DMA
    return pl.pallas_call(
        kernel,
        out_shape=(
            pltpu.VMEM((1, ROWS, HQ * HD), BF16),
            pltpu.VMEM((1, 256, HQ), F32),
            pltpu.VMEM((1, ROWS, WIDE), BF16),
        ),
        in_specs=[anywhere] * 7,
        out_specs=(local, local, local),
        scratch_shapes=[
            pltpu.VMEM((HQ, ROWS, HD), BF16),
            pltpu.VMEM((ROLES, ROWS, HK * HD), BF16),
            pltpu.VMEM((ROLES, ROWS, HK * HD), BF16),
            pltpu.VMEM((HQ, ROWS, ROLES * ROWS), F32),
            pltpu.VMEM((HQ, ROWS, ROWS), F32),
            pltpu.VMEM((HQ, ROWS, ROWS), F32),
            pltpu.VMEM((ROWS, ROWS), F32),
            pltpu.VMEM((LONG * PIECE, WIDE), BF16),
            pltpu.SMEM((1, 8), jnp.int32),
            pltpu.VMEM((32, 32), jnp.int32),
            pltpu.VMEM((32, 32), jnp.int32),
            pltpu.VMEM((2, 4, 8, ROWS), F32),
            pltpu.VMEM((2, 4, 8, ROWS), F32),
            pltpu.VMEM((4, 2, 8, ROWS), F32),
            pltpu.VMEM((4, 4, 2, 8, ROWS), F32),
            dma((HQ,)),
            dma((2,)),
            dma((3,)),
            dma((2, 12)),
            dma((2, ROLES)),
            dma((LONG + 1,)),
            dma((LONG + 1,)),
            dma((2 * LONG,)),
            dma((LONG,)),
            dma((7,)),
            dma((7,)),
        ],
        compiler_params=pltpu.CompilerParams(
            collective_id=0, has_side_effects=True, vmem_limit_bytes=52 << 20
        ),
    )(queries, keys, values, handoff, doc_lengths, task_lengths, assignment)


def solution(mesh):
    rows = P("section", "attn", None)
    small = P("section", None, None)
    return jax.shard_map(
        shards,
        mesh=mesh,
        in_specs=(rows, rows, rows, rows, P("section", None), small, small),
        out_specs=(rows, rows, rows),
        check_vma=False,
    )
```

```python
import math

import jax
import jax.numpy as jnp
from jax import lax
from jax.experimental import pallas as pl
from jax.experimental.pallas import tpu as pltpu
from jax.sharding import PartitionSpec as P

MESH = pl.DeviceIdType.MESH
F32 = jnp.float32
BF16 = jnp.bfloat16
HQ = 32
HK = 4
HD = 128
GROUP = HQ // HK
ROWS = 128
WIDE = 8192
ROLES = 9
LONG = 6
PIECE = 16
HALF = WIDE // 2
NEAR = 7
TAIL = 16
SCALE = HD ** -0.5
EXP2 = SCALE / math.log(2.0)


def section_of(z, core):
    return (z // 2) * 2 + core


def owner_of(y, z, x):
    return y * 8 + (z % 2) * 4 + x


def long_pieces(z):
    return jnp.where((z == 1) | (z == 4), 5, jnp.where((z == 2) | (z == 3), 3, 0))


def kernel(
    q_hbm, k_hbm, v_hbm, h_hbm, dl_hbm, tl_hbm, as_hbm,
    ctx, lse, rec,
    qs, kb, vb, sc, mx, mx2, top1, sum1, rl, rl2, stat, table, mid, ends, tl, ws,
    pack, t2, t3, turned,
    q_sem, own_sem, int_sem, kv_send, kv_recv, h_send, h_recv, m_send, m_recv,
    s_send, s_recv,
):
    s = lax.axis_index("section")
    a = lax.axis_index("attn")
    core = s % 2
    y = a // 8
    zl = (a // 4) % 2
    x = a % 4
    z = (s // 2) * 2 + zl
    up = (z + 3) % 8
    down = (z + 5) % 8
    right = a - x + (x + 1) % 4
    left = a - x + (x + 3) % 4

    sender = (core == 1) & (z < 6)
    own_long = jnp.where(core == 1, long_pieces(z), 0)
    mid_long = jnp.where(core == 0, long_pieces(up), 0)
    is_sender = own_long > 0
    is_mid = mid_long > 0
    last_long = jnp.where((core == 0) & (z >= 2), long_pieces((z + 6) % 8), 0)
    is_last = last_long > 0

    for h in range(HQ):
        pltpu.make_async_copy(
            q_hbm.at[0, :, pl.ds(h * HD, HD)], qs.at[h], q_sem.at[h]
        ).start()
    own = [
        pltpu.make_async_copy(k_hbm.at[0], kb.at[0], own_sem.at[0]),
        pltpu.make_async_copy(v_hbm.at[0], vb.at[0], own_sem.at[1]),
    ]
    ints = [
        pltpu.make_async_copy(dl_hbm, ends, int_sem.at[0]),
        pltpu.make_async_copy(tl_hbm.at[0], tl, int_sem.at[1]),
        pltpu.make_async_copy(as_hbm.at[0], ws, int_sem.at[2]),
    ]
    for copy in own + ints:
        copy.start()

    barrier = pltpu.get_barrier_semaphore()

    def greet(device):
        pl.semaphore_signal(barrier, inc=1, device_id=device, device_id_type=MESH)

    @pl.when(s > 0)
    def _():
        greet((s - 1, a))

    @pl.when(is_mid)
    def _():
        greet((section_of(up, 1), owner_of(y, up, x)))

    @pl.when(is_last)
    def _():
        greet((section_of(up, 0), owner_of(y, up, x)))

    @pl.when((zl == 0) & (y > 0))
    def _():
        greet((s, a - 4))

    plane = a - a % 8
    spot = a % 8
    for d in range(1, 8):
        greet((s, plane + (spot + d) % 8))
    for d in range(1, 4):
        greet((s, (a + 8 * d) % 32))
    expected = 10 + jnp.where(s < 7, 1, 0) + jnp.where(is_sender, 1, 0) + jnp.where(is_mid, 1, 0)
    expected = expected + jnp.where((zl == 1) & (y < 3), 1, 0)
    pl.semaphore_wait(barrier, expected)

    hbm = (k_hbm, v_hbm)
    buf = (kb, vb)

    def block(t, n, source, role, device):
        return pltpu.make_async_remote_copy(
            source, buf[t].at[role], kv_send.at[t, n], kv_recv.at[t, role],
            device_id=(s, device), device_id_type=MESH,
        )

    c_ok = (zl == 1) | (y > 0)
    odd = x % 2 == 1
    across = jnp.minimum(a + 4, 31)
    above = jnp.minimum(a + 8, 31)

    def transfers(t):
        return [
            (y < 3, block(t, 0, hbm[t].at[0], 1, above)),
            ((zl == 0) | (y < 3), block(t, 1, hbm[t].at[0], 2, across)),
            (x < 3, block(t, 2, hbm[t].at[0], 4, right)),
            (x == 0, block(t, 3, hbm[t].at[0], 3, left)),
            ((x == 3) & (y > 0), block(t, 4, buf[t].at[1], 4, right)),
            ((x > 0) & (y > 0), block(t, 5, buf[t].at[1], 3, left)),
            (c_ok, block(t, 6, buf[t].at[2], 6, right)),
            (c_ok, block(t, 7, buf[t].at[2], 5, left)),
            (odd & ((x == 3) | (y > 0)), block(t, 8, buf[t].at[3], 7, left)),
            ((x % 2 == 0) & ((x == 2) | (y > 0)), block(t, 9, buf[t].at[4], 7, right)),
            ((x % 2 == 0) & c_ok, block(t, 10, buf[t].at[5], 8, left)),
            (odd & c_ok, block(t, 11, buf[t].at[6], 8, right)),
        ]

    moves = (transfers(0), transfers(1))

    def send(t, *numbers):
        for n in numbers:
            cond, copy = moves[t][n]
            pl.when(cond)(copy.start)

    base = a - x

    def straight(other):
        return base + other - jnp.where(other > x, 8, 0)

    def crossed(other):
        return base - 4 + other

    xr, xl, xo = (x + 1) % 4, (x + 3) % 4, (x + 2) % 4
    owners = [
        a, a - 8, a - 4, straight(xr), straight(xl), crossed(xr), crossed(xl),
        straight(xo), crossed(xo),
    ]

    def arrive(t, role):
        @pl.when(owners[role] >= 0)
        def _():
            block(t, 0, hbm[t].at[0], role, a).wait_recv()

        @pl.when(owners[role] < 0)
        def _():
            buf[t][role] = jnp.zeros((ROWS, HK * HD), BF16)

    nxt = jnp.minimum(s + 1, 7)

    def direct(lo, rows, i):
        return pltpu.make_async_remote_copy(
            h_hbm.at[0, pl.ds(lo, rows)], rec.at[0, pl.ds(lo, rows)],
            h_send.at[i], h_recv.at[i], device_id=(nxt, a), device_id_type=MESH,
        )

    def part(i):
        return pl.ds((i // 2) * PIECE, PIECE), pl.ds((i % 2) * HALF, HALF)

    def piece(i):
        rows, lanes = part(i)
        return pltpu.make_async_remote_copy(
            h_hbm.at[0, rows, lanes], rec.at[0, rows, lanes],
            h_send.at[i], h_recv.at[i], device_id=(nxt, a), device_id_type=MESH,
        )

    late = ROWS - TAIL
    main = direct(LONG // 2 * PIECE, late - LONG // 2 * PIECE, LONG)
    rest = direct(late, TAIL, LONG + 1)
    held_back = (core == 1) & (zl == 0) & (s < 7)

    def leg1(i):
        rows, lanes = part(i)
        return pltpu.make_async_remote_copy(
            h_hbm.at[0, rows, lanes], mid.at[rows, lanes], m_send.at[i], m_recv.at[i],
            device_id=(section_of(down, 0), owner_of(y, down, x)), device_id_type=MESH,
        )

    def leg2(i):
        rows, lanes = part(i)
        return pltpu.make_async_remote_copy(
            mid.at[rows, lanes], rec.at[0, rows, lanes], m_send.at[LONG + i], h_recv.at[i],
            device_id=(section_of(down, 0), owner_of(y, down, x)), device_id_type=MESH,
        )

    def relay(i):
        @pl.when(mid_long > i)
        def _():
            leg1(i).wait_recv()
            leg2(i).start()

    send(0, 1, 0, 2, 3)
    send(1, 0, 2, 3)
    for i in range(2):
        pl.when(own_long > i)(leg1(i).start)
    send(1, 1)
    for i in range(2, LONG):
        pl.when(own_long > i)(leg1(i).start)

    @pl.when(s < 7)
    def _():
        main.start()

    for i in range(LONG):
        pl.when((s < 7) & (own_long <= i))(piece(i).start)
    pl.when((s < 7) & jnp.logical_not(held_back))(rest.start)

    @pl.when(s == 0)
    def _():
        rec[...] = jnp.zeros_like(rec)

    for copy in ints + own:
        copy.wait()

    row = lax.broadcasted_iota(jnp.int32, (ROWS, ROWS), 0)
    lane = lax.broadcasted_iota(jnp.int32, (ROWS, ROWS), 1)
    position = a * ROWS + row
    first = jnp.zeros((ROWS, ROWS), jnp.int32)
    end = jnp.int32(0)
    for i in range(8):
        end = end + ends[0, i]
        first = jnp.where(position >= end, end, first)

    for h in range(HQ):
        pltpu.make_async_copy(
            q_hbm.at[0, :, pl.ds(h * HD, HD)], qs.at[h], q_sem.at[h]
        ).wait()

    def scores(role, count, highest, fresh):
        bias = jnp.concatenate(
            [
                jnp.where(
                    (owners[r] * ROWS + lane >= first) & (owners[r] * ROWS + lane <= position),
                    F32(0), F32(-1e30),
                )
                for r in range(role, role + count)
            ],
            axis=1,
        )

        def body(g, carry):
            keys = kb[role:role + count, :, pl.ds(pl.multiple_of(g * HD, HD), HD)]
            heads = pl.ds(g * GROUP, GROUP)
            found = lax.dot_general(
                qs[heads].reshape(GROUP * ROWS, HD), keys.reshape(count * ROWS, HD),
                (((1,), (1,)), ((), ())), preferred_element_type=F32,
            ).reshape(GROUP, ROWS, count * ROWS) + bias[None]
            sc[heads, :, role * ROWS:(role + count) * ROWS] = found
            best = found[:, :, :ROWS]
            if count == 2:
                best = jnp.maximum(best, found[:, :, ROWS:])
            highest[heads] = best if fresh else jnp.maximum(highest[heads], best)
            return carry

        lax.fori_loop(0, HK, body, 0)

    near = NEAR * ROWS

    def soft_near(h, carry):
        top = jnp.max(mx[h], axis=1, keepdims=True)
        raised = jnp.exp2((sc[h, :, :near] - top) * F32(EXP2))
        sc[h, :, :near] = raised
        top1[h] = jnp.broadcast_to(top, (ROWS, ROWS))
        sum1[h] = jnp.broadcast_to(jnp.sum(raised, axis=1, keepdims=True), (ROWS, ROWS))
        return carry

    def soft_far(h, carry):
        top = jnp.max(mx2[h], axis=1, keepdims=True)
        raised = jnp.exp2((sc[h, :, near:] - top) * F32(EXP2))
        sc[h, :, near:] = raised
        total = jnp.sum(raised, axis=1, keepdims=True)
        before = top1[h]
        highest = jnp.maximum(before, top)
        lift1 = jnp.exp2((before - highest) * F32(EXP2))
        lift2 = jnp.exp2((top - highest) * F32(EXP2))
        total = sum1[h] * lift1 + total * lift2
        share = 1.0 / total
        rl[h] = lift1 * share
        rl2[h] = lift2 * share
        value = highest * F32(SCALE) + jnp.log(total)
        stat[...] = jnp.where(lane == h, value, stat[...])
        return carry

    def weighted(h, carry):
        factor = jnp.concatenate(
            [jnp.tile(rl[h], (1, NEAR)), jnp.tile(rl2[h], (1, ROLES - NEAR))], axis=1
        )
        weights = (sc[h] * factor).astype(BF16)
        lanes = pl.ds(pl.multiple_of((h // GROUP) * HD, HD), HD)
        rows = vb[:, :, lanes].reshape(ROLES * ROWS, HD)
        out = lax.dot_general(
            weights, rows, (((1,), (0,)), ((), ())), preferred_element_type=F32
        )
        ctx[0, :, pl.ds(pl.multiple_of(h * HD, HD), HD)] = out.astype(BF16)
        return carry

    def loop(body, low, high):
        lax.fori_loop(low, high, body, 0, unroll=2)

    scores(0, 1, mx, True)
    arrive(0, 1)
    send(0, 4, 5)
    arrive(0, 2)
    send(0, 6, 7)

    slots = lax.broadcasted_iota(jnp.int32, (256, 32), 0)
    tasks = lax.broadcasted_iota(jnp.int32, (256, 32), 1)
    lengths = tl[pl.ds(a, 1), :]
    workers = ws[pl.ds(a, 1), :]
    picked = workers == slots // 8
    which = jnp.sum(jnp.where(picked, tasks, 0), axis=1, keepdims=True)
    length = jnp.sum(jnp.where(picked, lengths, 0), axis=1, keepdims=True)
    start = jnp.sum(jnp.where(tasks < which, lengths, 0), axis=1, keepdims=True)
    rank = lax.broadcasted_iota(jnp.int32, (256, ROWS), 0) % 8
    token = lax.broadcasted_iota(jnp.int32, (256, ROWS), 1)
    table[...] = jnp.where((token == start + rank) & (rank < length), F32(1), F32(0))
    stat[...] = jnp.zeros_like(stat)

    scores(1, 2, mx, False)
    relay(0)
    arrive(0, 3)
    arrive(0, 4)
    send(0, 8, 9)
    arrive(1, 1)
    send(1, 4, 5)
    scores(3, 2, mx, False)
    relay(1)
    arrive(0, 5)
    arrive(0, 6)
    send(0, 10, 11)
    arrive(1, 2)
    send(1, 6, 7)
    scores(5, 2, mx, False)
    loop(soft_near, 0, 16)
    relay(2)
    arrive(1, 3)
    arrive(1, 4)
    send(1, 8, 9)
    loop(soft_near, 16, HQ)
    arrive(0, 7)
    arrive(0, 8)
    scores(7, 2, mx2, True)
    relay(3)
    arrive(1, 5)
    arrive(1, 6)
    send(1, 10, 11)
    loop(soft_far, 0, HQ)

    packed = jnp.zeros((64, ROWS), F32)
    for i in range(4):
        moved = stat[...] if i == 0 else pltpu.roll(stat[...], 32 * i, 1)
        packed = packed + lax.dot_general(
            table[i * 64:(i + 1) * 64], moved, (((1,), (0,)), ((), ())),
            precision=lax.Precision.HIGHEST, preferred_element_type=F32,
        )
    pack[...] = packed.reshape(8, 8, ROWS)
    stage1 = [
        pltpu.make_async_remote_copy(
            pack.at[(spot + d) % 8], t2.at[spot], s_send.at[d - 1], s_recv.at[d - 1],
            device_id=(s, plane + (spot + d) % 8), device_id_type=MESH,
        )
        for d in range(1, 8)
    ]
    for copy in stage1:
        copy.start()
    t2[pl.ds(spot, 1)] = pack[pl.ds(spot, 1)]
    pl.when(held_back)(rest.start)
    relay(4)

    for role in (7, 8):
        arrive(1, role)
    loop(weighted, 0, 16)
    for copy in stage1:
        copy.wait()
    stage2 = [
        pltpu.make_async_remote_copy(
            t2, t3.at[y], s_send.at[6 + d], s_recv.at[6 + d],
            device_id=(s, (a + 8 * d) % 32), device_id_type=MESH,
        )
        for d in range(1, 4)
    ]
    for copy in stage2:
        copy.start()
    t3[pl.ds(y, 1)] = t2[...].reshape(1, 8, 8, ROWS)
    loop(weighted, 16, HQ)
    for copy in stage2:
        copy.wait()
    turned[...] = t3[...].reshape(256, ROWS).T
    lse[0] = turned[pl.ds(pl.multiple_of(y * HQ, HQ), HQ), :]

    for t in range(2):
        for cond, copy in moves[t]:
            pl.when(cond)(copy.wait_send)
    for i in range(LONG):
        pl.when(own_long > i)(leg1(i).wait_send)
        pl.when(mid_long > i)(leg2(i).wait_send)
        pl.when((s < 7) & (own_long <= i))(piece(i).wait_send)

    @pl.when(s < 7)
    def _():
        main.wait_send()
        rest.wait_send()

    @pl.when(s > 0)
    def _():
        for i in range(LONG):
            piece(i).wait_recv()
        main.wait_recv()
        rest.wait_recv()


def deliver(*refs):
    count = len(refs) // 2
    sems = refs[-1]
    copies = [
        pltpu.make_async_copy(refs[i], refs[count + i], sems.at[i]) for i in range(count)
    ]
    for copy in copies:
        copy.start()
    for copy in copies:
        copy.wait()


def shards(queries, keys, values, handoff, doc_lengths, task_lengths, assignment):
    anywhere = pl.BlockSpec(memory_space=pltpu.HBM)
    local = pl.BlockSpec(memory_space=pltpu.VMEM)
    dma = pltpu.SemaphoreType.DMA
    results = pl.pallas_call(
        kernel,
        out_shape=(
            pltpu.VMEM((1, ROWS, HQ * HD), BF16),
            pltpu.VMEM((1, HQ, 256), F32),
            pltpu.VMEM((1, ROWS, WIDE), BF16),
        ),
        in_specs=[anywhere] * 7,
        out_specs=(local, local, local),
        scratch_shapes=[
            pltpu.VMEM((HQ, ROWS, HD), BF16),
            pltpu.VMEM((ROLES, ROWS, HK * HD), BF16),
            pltpu.VMEM((ROLES, ROWS, HK * HD), BF16),
            pltpu.VMEM((HQ, ROWS, ROLES * ROWS), F32),
            *[pltpu.VMEM((HQ, ROWS, ROWS), F32)] * 6,
            pltpu.VMEM((ROWS, ROWS), F32),
            pltpu.VMEM((256, ROWS), F32),
            pltpu.VMEM((LONG // 2 * PIECE, WIDE), BF16),
            pltpu.SMEM((1, 8), jnp.int32),
            pltpu.VMEM((32, 32), jnp.int32),
            pltpu.VMEM((32, 32), jnp.int32),
            pltpu.VMEM((8, 8, ROWS), F32),
            pltpu.VMEM((8, 8, ROWS), F32),
            pltpu.VMEM((4, 8, 8, ROWS), F32),
            pltpu.VMEM((ROWS, 256), F32),
            dma((HQ,)),
            dma((2,)),
            dma((3,)),
            dma((2, 12)),
            dma((2, ROLES)),
            dma((LONG + 2,)),
            dma((LONG + 2,)),
            dma((2 * LONG,)),
            dma((LONG,)),
            dma((10,)),
            dma((10,)),
        ],
        compiler_params=pltpu.CompilerParams(
            collective_id=0, has_side_effects=True, vmem_limit_bytes=52 << 20
        ),
    )(queries, keys, values, handoff, doc_lengths, task_lengths, assignment)
    context, stats, received = pl.pallas_call(
        deliver,
        out_shape=tuple(jax.ShapeDtypeStruct(r.shape, r.dtype) for r in results),
        in_specs=[local] * 3,
        out_specs=(anywhere,) * 3,
        scratch_shapes=[dma((3,))],
    )(*[pltpu.with_memory_space_constraint(r, pltpu.VMEM) for r in results])
    return context, jnp.swapaxes(stats, 1, 2), received


def solution(mesh):
    rows = P("section", "attn", None)
    small = P("section", None, None)
    return jax.shard_map(
        shards,
        mesh=mesh,
        in_specs=(rows, rows, rows, rows, P("section", None), small, small),
        out_specs=(rows, rows, rows),
        check_vma=False,
    )
```

```python
import math

import jax
import jax.numpy as jnp
from jax import lax
from jax.experimental import pallas as pl
from jax.experimental.pallas import tpu as pltpu
from jax.sharding import PartitionSpec as P

MESH = pl.DeviceIdType.MESH
F32 = jnp.float32
BF16 = jnp.bfloat16
HQ = 32
HK = 4
HD = 128
GROUP = HQ // HK
ROWS = 128
WIDE = 8192
ROLES = 9
LONG = 6
PIECE = 16
HALF = WIDE // 2
NEAR = 7
NEAR_HEADS = 4
FAR_HEADS = 8
TAIL = 16
SCALE = HD ** -0.5
EXP2 = SCALE / math.log(2.0)


def section_of(z, core):
    return (z // 2) * 2 + core


def owner_of(y, z, x):
    return y * 8 + (z % 2) * 4 + x


def long_pieces(z):
    return jnp.where((z == 1) | (z == 4), 5, jnp.where((z == 2) | (z == 3), 3, 0))


def kernel(
    q_hbm, k_hbm, v_hbm, h_hbm, dl_hbm, tl_hbm, as_hbm,
    ctx, lse, rec,
    qs, kb, vb, sc, mx, mx2, top1, sum1, rl, rl2, stat, table, mid, ends, tl, ws,
    pack, t2,
    q_sem, own_sem, int_sem, kv_send, kv_recv, h_send, h_recv, m_send, m_recv,
    s_send, s_recv, ready,
):
    s = lax.axis_index("section")
    a = lax.axis_index("attn")
    core = s % 2
    y = a // 8
    zl = (a // 4) % 2
    x = a % 4
    z = (s // 2) * 2 + zl
    up = (z + 3) % 8
    down = (z + 5) % 8
    right = a - x + (x + 1) % 4
    left = a - x + (x + 3) % 4

    sender = (core == 1) & (z < 6)
    own_long = jnp.where(core == 1, long_pieces(z), 0)
    mid_long = jnp.where(core == 1, long_pieces(up), 0)
    is_sender = own_long > 0
    is_mid = mid_long > 0
    last_long = jnp.where((core == 0) & (z >= 2), long_pieces((z + 6) % 8), 0)
    is_last = last_long > 0

    barrier = pltpu.get_barrier_semaphore()

    def greet(device):
        pl.semaphore_signal(barrier, inc=1, device_id=device, device_id_type=MESH)

    @pl.when(s > 0)
    def _():
        greet((s - 1, a))

    @pl.when(is_mid)
    def _():
        greet((section_of(up, 1), owner_of(y, up, x)))

    @pl.when(is_last)
    def _():
        greet((section_of(up, 1), owner_of(y, up, x)))

    @pl.when((zl == 0) & (y > 0))
    def _():
        greet((s, a - 4))

    plane = a - a % 8
    spot = a % 8
    for d in range(1, 8):
        greet((s, plane + (spot + d) % 8))
    for d in range(1, 4):
        greet((s, (a + 8 * d) % 32))
    expected = 10 + jnp.where(s < 7, 1, 0) + jnp.where(is_sender, 1, 0) + jnp.where(is_mid, 1, 0)
    expected = expected + jnp.where((zl == 1) & (y < 3), 1, 0)
    for h in range(HQ):
        pltpu.make_async_copy(
            q_hbm.at[0, :, pl.ds(h * HD, HD)], qs.at[h], q_sem.at[h]
        ).start()
    own = [
        pltpu.make_async_copy(k_hbm.at[0], kb.at[0], own_sem.at[0]),
        pltpu.make_async_copy(v_hbm.at[0], vb.at[0], own_sem.at[1]),
    ]
    ints = [
        pltpu.make_async_copy(dl_hbm, ends, int_sem.at[0]),
        pltpu.make_async_copy(tl_hbm.at[0], tl, int_sem.at[1]),
        pltpu.make_async_copy(as_hbm.at[0], ws, int_sem.at[2]),
    ]
    for copy in own + ints:
        copy.start()

    pl.semaphore_wait(barrier, expected)

    hbm = (k_hbm, v_hbm)
    buf = (kb, vb)

    def block(t, n, source, role, device):
        return pltpu.make_async_remote_copy(
            source, buf[t].at[role], kv_send.at[t, n], kv_recv.at[t, role],
            device_id=(s, device), device_id_type=MESH,
        )

    c_ok = (zl == 1) | (y > 0)
    odd = x % 2 == 1
    across = jnp.minimum(a + 4, 31)
    above = jnp.minimum(a + 8, 31)

    def transfers(t):
        return [
            (y < 3, block(t, 0, hbm[t].at[0], 1, above)),
            ((zl == 0) | (y < 3), block(t, 1, hbm[t].at[0], 2, across)),
            (x < 3, block(t, 2, hbm[t].at[0], 4, right)),
            (x == 0, block(t, 3, hbm[t].at[0], 3, left)),
            ((x == 3) & (y > 0), block(t, 4, buf[t].at[1], 4, right)),
            ((x > 0) & (y > 0), block(t, 5, buf[t].at[1], 3, left)),
            (c_ok, block(t, 6, buf[t].at[2], 6, right)),
            (c_ok, block(t, 7, buf[t].at[2], 5, left)),
            (odd & ((x == 3) | (y > 0)), block(t, 8, buf[t].at[3], 7, left)),
            ((x % 2 == 0) & ((x == 2) | (y > 0)), block(t, 9, buf[t].at[4], 7, right)),
            ((x % 2 == 0) & c_ok, block(t, 10, buf[t].at[5], 8, left)),
            (odd & c_ok, block(t, 11, buf[t].at[6], 8, right)),
        ]

    moves = (transfers(0), transfers(1))

    def send(t, *numbers):
        for n in numbers:
            cond, copy = moves[t][n]
            pl.when(cond)(copy.start)

    base = a - x

    def straight(other):
        return base + other - jnp.where(other > x, 8, 0)

    def crossed(other):
        return base - 4 + other

    xr, xl, xo = (x + 1) % 4, (x + 3) % 4, (x + 2) % 4
    owners = [
        a, a - 8, a - 4, straight(xr), straight(xl), crossed(xr), crossed(xl),
        straight(xo), crossed(xo),
    ]

    def arrive(t, role):
        @pl.when(owners[role] >= 0)
        def _():
            block(t, 0, hbm[t].at[0], role, a).wait_recv()

        @pl.when(owners[role] < 0)
        def _():
            buf[t][role] = jnp.zeros((ROWS, HK * HD), BF16)

    nxt = jnp.minimum(s + 1, 7)

    def direct(lo, rows, i):
        return pltpu.make_async_remote_copy(
            h_hbm.at[0, pl.ds(lo, rows)], rec.at[0, pl.ds(lo, rows)],
            h_send.at[i], h_recv.at[i], device_id=(nxt, a), device_id_type=MESH,
        )

    def part(i):
        return pl.ds((i // 2) * PIECE, PIECE), pl.ds((i % 2) * HALF, HALF)

    def piece(i):
        rows, lanes = part(i)
        return pltpu.make_async_remote_copy(
            h_hbm.at[0, rows, lanes], rec.at[0, rows, lanes],
            h_send.at[i], h_recv.at[i], device_id=(nxt, a), device_id_type=MESH,
        )

    late = ROWS - TAIL
    main = direct(LONG // 2 * PIECE, late - LONG // 2 * PIECE, LONG)
    rest = direct(late, TAIL, LONG + 1)
    held_back = (core == 1) & (zl == 0) & (s < 7)

    def leg1(i):
        rows, lanes = part(i)
        return pltpu.make_async_remote_copy(
            h_hbm.at[0, rows, lanes], mid.at[rows, lanes], m_send.at[i], m_recv.at[i],
            device_id=(section_of(down, 1), owner_of(y, down, x)), device_id_type=MESH,
        )

    def leg2(i):
        rows, lanes = part(i)
        return pltpu.make_async_remote_copy(
            mid.at[rows, lanes], rec.at[0, rows, lanes], m_send.at[LONG + i], h_recv.at[i],
            device_id=(section_of(down, 0), owner_of(y, down, x)), device_id_type=MESH,
        )

    def relay(i):
        @pl.when(mid_long > i)
        def _():
            leg1(i).wait_recv()
            leg2(i).start()

    send(0, 1, 0, 2, 3)
    send(1, 1, 0, 2, 3)
    for i in range(LONG):
        pl.when(own_long > i)(leg1(i).start)

    @pl.when(s < 7)
    def _():
        main.start()

    for i in range(LONG):
        pl.when((s < 7) & (own_long <= i))(piece(i).start)
    pl.when((s < 7) & jnp.logical_not(held_back))(rest.start)

    @pl.when(s == 0)
    def _():
        rec[...] = jnp.zeros_like(rec)

    for copy in ints + own:
        copy.wait()

    row = lax.broadcasted_iota(jnp.int32, (ROWS, ROWS), 0)
    lane = lax.broadcasted_iota(jnp.int32, (ROWS, ROWS), 1)
    position = a * ROWS + row
    first = jnp.zeros((ROWS, ROWS), jnp.int32)
    end = jnp.int32(0)
    for i in range(8):
        end = end + ends[0, i]
        first = jnp.where(position >= end, end, first)

    for h in range(HQ):
        pltpu.make_async_copy(
            q_hbm.at[0, :, pl.ds(h * HD, HD)], qs.at[h], q_sem.at[h]
        ).wait()

    def scores(role, count, highest, fresh):
        bias = jnp.concatenate(
            [
                jnp.where(
                    (owners[r] * ROWS + lane >= first) & (owners[r] * ROWS + lane <= position),
                    F32(0), F32(-1e30),
                )
                for r in range(role, role + count)
            ],
            axis=1,
        )

        def body(g, carry):
            keys = kb[role:role + count, :, pl.ds(pl.multiple_of(g * HD, HD), HD)]
            heads = pl.ds(g * GROUP, GROUP)
            found = lax.dot_general(
                qs[heads].reshape(GROUP * ROWS, HD), keys.reshape(count * ROWS, HD),
                (((1,), (1,)), ((), ())), preferred_element_type=F32,
            ).reshape(GROUP, ROWS, count * ROWS) + bias[None]
            sc[heads, :, role * ROWS:(role + count) * ROWS] = found
            best = found[:, :, :ROWS]
            if count == 2:
                best = jnp.maximum(best, found[:, :, ROWS:])
            highest[heads] = best if fresh else jnp.maximum(highest[heads], best)
            return carry

        lax.fori_loop(0, HK, body, 0)

    near = NEAR * ROWS

    def soft_near(h, carry):
        top = jnp.max(mx[h], axis=1, keepdims=True)
        raised = jnp.exp2((sc[h, :, :near] - top) * F32(EXP2))
        sc[h, :, :near] = raised
        top1[h] = jnp.broadcast_to(top, (ROWS, ROWS))
        sum1[h] = jnp.broadcast_to(jnp.sum(raised, axis=1, keepdims=True), (ROWS, ROWS))
        return carry

    def soft_far(h, carry):
        top = jnp.max(mx2[h], axis=1, keepdims=True)
        raised = jnp.exp2((sc[h, :, near:] - top) * F32(EXP2))
        sc[h, :, near:] = raised
        total = jnp.sum(raised, axis=1, keepdims=True)
        before = top1[h]
        highest = jnp.maximum(before, top)
        lift1 = jnp.exp2((before - highest) * F32(EXP2))
        lift2 = jnp.exp2((top - highest) * F32(EXP2))
        total = sum1[h] * lift1 + total * lift2
        share = 1.0 / total
        rl[h] = lift1 * share
        rl2[h] = lift2 * share
        value = highest * F32(SCALE) + jnp.log(total)
        stat[...] = jnp.where(lane == h, value, stat[...])
        return carry

    def weighted(step, heads, low, high, factor):
        chosen = pl.ds(step * heads, heads)
        lift = jnp.tile(factor[chosen], (1, 1, high - low))
        weights = (sc[chosen, :, low * ROWS:high * ROWS] * lift).astype(BF16)
        lanes = pl.ds(pl.multiple_of((step * heads // GROUP) * HD, HD), HD)
        rows = vb[low:high, :, lanes].reshape((high - low) * ROWS, HD)
        return lax.dot_general(
            weights.reshape(heads * ROWS, (high - low) * ROWS), rows,
            (((1,), (0,)), ((), ())), preferred_element_type=F32,
        ).reshape(heads, ROWS, HD)

    def weighted_near(step, carry):
        top1[pl.ds(step * NEAR_HEADS, NEAR_HEADS)] = weighted(step, NEAR_HEADS, 0, NEAR, rl)
        return carry

    def weighted_far(step, carry):
        out = weighted(step, FAR_HEADS, NEAR, ROLES, rl2)
        out = (out + top1[pl.ds(step * FAR_HEADS, FAR_HEADS)]).astype(BF16)
        for i in range(FAR_HEADS):
            ctx[0, :, pl.ds(pl.multiple_of((step * FAR_HEADS + i) * HD, HD), HD)] = out[i]
        return carry

    def loop(body, low, high):
        lax.fori_loop(low, high, body, 0, unroll=4)

    for d in range(1, 4):
        pl.semaphore_signal(
            ready, inc=1, device_id=(s, (a + 8 * d) % 32), device_id_type=MESH
        )

    scores(0, 1, mx, True)
    arrive(0, 1)
    send(0, 4, 5)
    arrive(0, 2)
    send(0, 6, 7)

    slots = lax.broadcasted_iota(jnp.int32, (256, 32), 0)
    slot_rank = slots // 64 + 4 * (slots % 2)
    tasks = lax.broadcasted_iota(jnp.int32, (256, 32), 1)
    lengths = tl[pl.ds(a, 1), :]
    workers = ws[pl.ds(a, 1), :]
    picked = workers == slots % 64 // 2
    which = jnp.sum(jnp.where(picked, tasks, 0), axis=1, keepdims=True)
    length = jnp.sum(jnp.where(picked, lengths, 0), axis=1, keepdims=True)
    start = jnp.sum(jnp.where(tasks < which, lengths, 0), axis=1, keepdims=True)
    rank = slot_rank[:, :1]
    token = lax.broadcasted_iota(jnp.int32, (256, ROWS), 1)
    table[...] = jnp.where((token == start + rank) & (rank < length), F32(1), F32(0))
    stat[...] = jnp.zeros_like(stat)

    scores(1, 2, mx, False)
    relay(0)
    arrive(0, 3)
    arrive(0, 4)
    send(0, 8, 9)
    arrive(1, 1)
    send(1, 4, 5)
    scores(3, 2, mx, False)
    relay(1)
    arrive(0, 5)
    arrive(0, 6)
    send(0, 10, 11)
    arrive(1, 2)
    send(1, 6, 7)
    scores(5, 2, mx, False)
    loop(soft_near, 0, 16)
    relay(2)
    arrive(1, 3)
    arrive(1, 4)
    send(1, 8, 9)
    loop(soft_near, 16, HQ)
    arrive(0, 7)
    arrive(0, 8)
    scores(7, 2, mx2, True)
    relay(3)
    arrive(1, 5)
    arrive(1, 6)
    send(1, 10, 11)
    loop(soft_far, 0, HQ)

    pl.semaphore_wait(ready, 3)
    packed = jnp.zeros((64, ROWS), F32)
    for i in range(4):
        moved = stat[...] if i == 0 else pltpu.roll(stat[...], 32 * i, 1)
        packed = packed + lax.dot_general(
            table[i * 64:(i + 1) * 64], moved, (((1,), (0,)), ((), ())),
            precision=lax.Precision.HIGHEST, preferred_element_type=F32,
        )
    pack[...] = packed.reshape(32, 2, ROWS)
    tasks_out = [
        pltpu.make_async_remote_copy(
            pack.at[(a + d) % 32], t2.at[a], s_send.at[d - 1], s_recv.at[d - 1],
            device_id=(s, (a + d) % 32), device_id_type=MESH,
        )
        for d in range(1, 32)
    ]
    for copy in tasks_out:
        copy.start()
    t2[pl.ds(a, 1)] = pack[pl.ds(a, 1)]
    pl.when(held_back)(rest.start)
    relay(4)

    lax.fori_loop(0, HQ // NEAR_HEADS, weighted_near, 0)
    for role in (7, 8):
        arrive(1, role)
    lax.fori_loop(0, HQ // FAR_HEADS, weighted_far, 0)
    for copy in tasks_out:
        copy.wait()
    turned = t2[...].reshape(64, ROWS).T
    turned = jnp.concatenate([turned[32 * i:32 * (i + 1)] for i in range(4)], axis=1)
    source = lax.broadcasted_iota(jnp.int32, (256, 256), 0)
    slot = lax.broadcasted_iota(jnp.int32, (256, 256), 1)
    spread = jnp.where(slot == 4 * (source % 64) + source // 64, F32(1), F32(0))
    lse[0] = lax.dot_general(
        turned, spread, (((1,), (0,)), ((), ())),
        precision=lax.Precision.HIGHEST, preferred_element_type=F32,
    )

    for t in range(2):
        for cond, copy in moves[t]:
            pl.when(cond)(copy.wait_send)
    for i in range(LONG):
        pl.when(own_long > i)(leg1(i).wait_send)
        pl.when(mid_long > i)(leg2(i).wait_send)
        pl.when((s < 7) & (own_long <= i))(piece(i).wait_send)

    @pl.when(s < 7)
    def _():
        main.wait_send()
        rest.wait_send()

    @pl.when(s > 0)
    def _():
        for i in range(LONG):
            piece(i).wait_recv()
        main.wait_recv()
        rest.wait_recv()


def deliver(*refs):
    count = len(refs) // 2
    sems = refs[-1]
    copies = [
        pltpu.make_async_copy(refs[i], refs[count + i], sems.at[i]) for i in range(count)
    ]
    for copy in copies:
        copy.start()
    for copy in copies:
        copy.wait()


def shards(queries, keys, values, handoff, doc_lengths, task_lengths, assignment):
    anywhere = pl.BlockSpec(memory_space=pltpu.HBM)
    local = pl.BlockSpec(memory_space=pltpu.VMEM)
    dma = pltpu.SemaphoreType.DMA
    results = pl.pallas_call(
        kernel,
        out_shape=(
            pltpu.VMEM((1, ROWS, HQ * HD), BF16),
            pltpu.VMEM((1, HQ, 256), F32),
            pltpu.VMEM((1, ROWS, WIDE), BF16),
        ),
        in_specs=[anywhere] * 7,
        out_specs=(local, local, local),
        scratch_shapes=[
            pltpu.VMEM((HQ, ROWS, HD), BF16),
            pltpu.VMEM((ROLES, ROWS, HK * HD), BF16),
            pltpu.VMEM((ROLES, ROWS, HK * HD), BF16),
            pltpu.VMEM((HQ, ROWS, ROLES * ROWS), F32),
            *[pltpu.VMEM((HQ, ROWS, ROWS), F32)] * 6,
            pltpu.VMEM((ROWS, ROWS), F32),
            pltpu.VMEM((256, ROWS), F32),
            pltpu.VMEM((LONG // 2 * PIECE, WIDE), BF16),
            pltpu.SMEM((1, 8), jnp.int32),
            pltpu.VMEM((32, 32), jnp.int32),
            pltpu.VMEM((32, 32), jnp.int32),
            pltpu.VMEM((32, 2, ROWS), F32),
            pltpu.VMEM((32, 2, ROWS), F32),
            dma((HQ,)),
            dma((2,)),
            dma((3,)),
            dma((2, 12)),
            dma((2, ROLES)),
            dma((LONG + 2,)),
            dma((LONG + 2,)),
            dma((2 * LONG,)),
            dma((LONG,)),
            dma((31,)),
            dma((31,)),
            pltpu.SemaphoreType.REGULAR,
        ],
        compiler_params=pltpu.CompilerParams(
            collective_id=0, has_side_effects=True, vmem_limit_bytes=52 << 20
        ),
    )(queries, keys, values, handoff, doc_lengths, task_lengths, assignment)
    context, stats, received = pl.pallas_call(
        deliver,
        out_shape=tuple(jax.ShapeDtypeStruct(r.shape, r.dtype) for r in results),
        in_specs=[local] * 3,
        out_specs=(anywhere,) * 3,
        scratch_shapes=[dma((3,))],
    )(*[pltpu.with_memory_space_constraint(r, pltpu.VMEM) for r in results])
    return context, jnp.swapaxes(stats, 1, 2), received


def solution(mesh):
    rows = P("section", "attn", None)
    small = P("section", None, None)
    return jax.shard_map(
        shards,
        mesh=mesh,
        in_specs=(rows, rows, rows, rows, P("section", None), small, small),
        out_specs=(rows, rows, rows),
        check_vma=False,
    )
```

```python
import math

import jax
import jax.numpy as jnp
from jax import lax
from jax.experimental import pallas as pl
from jax.experimental.pallas import tpu as pltpu
from jax.sharding import PartitionSpec as P

MESH = pl.DeviceIdType.MESH
F32 = jnp.float32
BF16 = jnp.bfloat16
HQ = 32
HK = 4
HD = 128
GROUP = HQ // HK
ROWS = 128
WIDE = 8192
ROLES = 9
LONG = 6
PIECE = 16
HALF = WIDE // 2
NEAR = 7
NEAR_HEADS = 4
FAR_HEADS = 8
TAIL = 16
SCALE = HD ** -0.5
EXP2 = SCALE / math.log(2.0)


def section_of(z, core):
    return (z // 2) * 2 + core


def owner_of(y, z, x):
    return y * 8 + (z % 2) * 4 + x


def long_pieces(z):
    return jnp.where((z == 1) | (z == 4), 5, jnp.where((z == 2) | (z == 3), 3, 0))


def kernel(
    q_hbm, k_hbm, v_hbm, h_hbm, dl_hbm, tl_hbm, as_hbm,
    ctx, lse, rec,
    qs, kb, vb, sc, mx, mx2, top1, sum1, rl, rl2, stat, table, mid, ends, tl, ws,
    pack, t2,
    q_sem, own_sem, int_sem, kv_send, kv_recv, h_send, h_recv, m_send, m_recv,
    s_send, s_recv, ready, met,
):
    s = lax.axis_index("section")
    a = lax.axis_index("attn")
    core = s % 2
    y = a // 8
    zl = (a // 4) % 2
    x = a % 4
    z = (s // 2) * 2 + zl
    up = (z + 3) % 8
    down = (z + 5) % 8
    right = a - x + (x + 1) % 4
    left = a - x + (x + 3) % 4

    sender = (core == 1) & (z < 6)
    own_long = jnp.where(core == 1, long_pieces(z), 0)
    mid_long = jnp.where(core == 1, long_pieces(up), 0)
    is_sender = own_long > 0
    is_mid = mid_long > 0
    last_long = jnp.where((core == 0) & (z >= 2), long_pieces((z + 6) % 8), 0)
    is_last = last_long > 0

    barrier = pltpu.get_barrier_semaphore()

    def greet(device):
        pl.semaphore_signal(barrier, inc=1, device_id=device, device_id_type=MESH)

    @pl.when(s > 0)
    def _():
        greet((s - 1, a))

    @pl.when(is_mid)
    def _():
        greet((section_of(up, 1), owner_of(y, up, x)))

    @pl.when(is_last)
    def _():
        greet((section_of(up, 1), owner_of(y, up, x)))

    @pl.when((zl == 0) & (y > 0))
    def _():
        greet((s, a - 4))

    plane = a - a % 8
    spot = a % 8
    partner = plane + (spot + 4) % 8
    greet((s, partner))
    for d in range(1, 4):
        greet((s, a - x + (x + d) % 4))
    for d in range(1, 4):
        greet((s, (a + 8 * d) % 32))
    expected = 7 + jnp.where(s < 7, 1, 0) + jnp.where(is_sender, 1, 0) + jnp.where(is_mid, 1, 0)
    expected = expected + jnp.where((zl == 1) & (y < 3), 1, 0)
    for h in range(HQ):
        pltpu.make_async_copy(
            q_hbm.at[0, :, pl.ds(h * HD, HD)], qs.at[h], q_sem.at[h]
        ).start()
    own = [
        pltpu.make_async_copy(k_hbm.at[0], kb.at[0], own_sem.at[0]),
        pltpu.make_async_copy(v_hbm.at[0], vb.at[0], own_sem.at[1]),
    ]
    ints = [
        pltpu.make_async_copy(dl_hbm, ends, int_sem.at[0]),
        pltpu.make_async_copy(tl_hbm.at[0], tl, int_sem.at[1]),
        pltpu.make_async_copy(as_hbm.at[0], ws, int_sem.at[2]),
    ]
    for copy in own + ints:
        copy.start()

    pl.semaphore_wait(barrier, expected)

    pl.semaphore_signal(met, inc=1, device_id=(s, partner), device_id_type=MESH)

    hbm = (k_hbm, v_hbm)
    buf = (kb, vb)

    def block(t, n, source, role, device):
        return pltpu.make_async_remote_copy(
            source, buf[t].at[role], kv_send.at[t, n], kv_recv.at[t, role],
            device_id=(s, device), device_id_type=MESH,
        )

    c_ok = (zl == 1) | (y > 0)
    odd = x % 2 == 1
    across = jnp.minimum(a + 4, 31)
    above = jnp.minimum(a + 8, 31)

    def transfers(t):
        return [
            (y < 3, block(t, 0, hbm[t].at[0], 1, above)),
            ((zl == 0) | (y < 3), block(t, 1, hbm[t].at[0], 2, across)),
            (x < 3, block(t, 2, hbm[t].at[0], 4, right)),
            (x == 0, block(t, 3, hbm[t].at[0], 3, left)),
            ((x == 3) & (y > 0), block(t, 4, buf[t].at[1], 4, right)),
            ((x > 0) & (y > 0), block(t, 5, buf[t].at[1], 3, left)),
            (c_ok, block(t, 6, buf[t].at[2], 6, right)),
            (c_ok, block(t, 7, buf[t].at[2], 5, left)),
            (odd & ((x == 3) | (y > 0)), block(t, 8, buf[t].at[3], 7, left)),
            ((x % 2 == 0) & ((x == 2) | (y > 0)), block(t, 9, buf[t].at[4], 7, right)),
            ((x % 2 == 0) & c_ok, block(t, 10, buf[t].at[5], 8, left)),
            (odd & c_ok, block(t, 11, buf[t].at[6], 8, right)),
        ]

    moves = (transfers(0), transfers(1))

    def send(t, *numbers):
        for n in numbers:
            cond, copy = moves[t][n]
            pl.when(cond)(copy.start)

    base = a - x

    def straight(other):
        return base + other - jnp.where(other > x, 8, 0)

    def crossed(other):
        return base - 4 + other

    xr, xl, xo = (x + 1) % 4, (x + 3) % 4, (x + 2) % 4
    owners = [
        a, a - 8, a - 4, straight(xr), straight(xl), crossed(xr), crossed(xl),
        straight(xo), crossed(xo),
    ]

    def arrive(t, role):
        @pl.when(owners[role] >= 0)
        def _():
            block(t, 0, hbm[t].at[0], role, a).wait_recv()

        @pl.when(owners[role] < 0)
        def _():
            buf[t][role] = jnp.zeros((ROWS, HK * HD), BF16)

    nxt = jnp.minimum(s + 1, 7)

    def direct(lo, rows, i):
        return pltpu.make_async_remote_copy(
            h_hbm.at[0, pl.ds(lo, rows)], rec.at[0, pl.ds(lo, rows)],
            h_send.at[i], h_recv.at[i], device_id=(nxt, a), device_id_type=MESH,
        )

    def part(i):
        return pl.ds((i // 2) * PIECE, PIECE), pl.ds((i % 2) * HALF, HALF)

    def piece(i):
        rows, lanes = part(i)
        return pltpu.make_async_remote_copy(
            h_hbm.at[0, rows, lanes], rec.at[0, rows, lanes],
            h_send.at[i], h_recv.at[i], device_id=(nxt, a), device_id_type=MESH,
        )

    late = ROWS - TAIL
    main = direct(LONG // 2 * PIECE, late - LONG // 2 * PIECE, LONG)
    rest = direct(late, TAIL, LONG + 1)
    held_back = (core == 1) & (zl == 0) & (s < 7)

    def leg1(i):
        rows, lanes = part(i)
        return pltpu.make_async_remote_copy(
            h_hbm.at[0, rows, lanes], mid.at[rows, lanes], m_send.at[i], m_recv.at[i],
            device_id=(section_of(down, 1), owner_of(y, down, x)), device_id_type=MESH,
        )

    def leg2(i):
        rows, lanes = part(i)
        return pltpu.make_async_remote_copy(
            mid.at[rows, lanes], rec.at[0, rows, lanes], m_send.at[LONG + i], h_recv.at[i],
            device_id=(section_of(down, 0), owner_of(y, down, x)), device_id_type=MESH,
        )

    def relay(i):
        @pl.when(mid_long > i)
        def _():
            leg1(i).wait_recv()
            leg2(i).start()

    send(0, 1, 0, 2, 3)
    send(1, 1, 0, 2, 3)
    for i in range(LONG):
        pl.when(own_long > i)(leg1(i).start)

    @pl.when(s < 7)
    def _():
        main.start()

    for i in range(LONG):
        pl.when((s < 7) & (own_long <= i))(piece(i).start)
    pl.when((s < 7) & jnp.logical_not(held_back))(rest.start)

    @pl.when(s == 0)
    def _():
        rec[...] = jnp.zeros_like(rec)

    for copy in ints + own:
        copy.wait()

    row = lax.broadcasted_iota(jnp.int32, (ROWS, ROWS), 0)
    lane = lax.broadcasted_iota(jnp.int32, (ROWS, ROWS), 1)
    position = a * ROWS + row
    first = jnp.zeros((ROWS, ROWS), jnp.int32)
    end = jnp.int32(0)
    for i in range(8):
        end = end + ends[0, i]
        first = jnp.where(position >= end, end, first)

    for h in range(HQ):
        pltpu.make_async_copy(
            q_hbm.at[0, :, pl.ds(h * HD, HD)], qs.at[h], q_sem.at[h]
        ).wait()

    def scores(role, count, highest, fresh):
        bias = jnp.concatenate(
            [
                jnp.where(
                    (owners[r] * ROWS + lane >= first) & (owners[r] * ROWS + lane <= position),
                    F32(0), F32(-1e30),
                )
                for r in range(role, role + count)
            ],
            axis=1,
        )

        def body(g, carry):
            keys = kb[role:role + count, :, pl.ds(pl.multiple_of(g * HD, HD), HD)]
            heads = pl.ds(g * GROUP, GROUP)
            found = lax.dot_general(
                qs[heads].reshape(GROUP * ROWS, HD), keys.reshape(count * ROWS, HD),
                (((1,), (1,)), ((), ())), preferred_element_type=F32,
            ).reshape(GROUP, ROWS, count * ROWS) + bias[None]
            sc[heads, :, role * ROWS:(role + count) * ROWS] = found
            best = found[:, :, :ROWS]
            if count == 2:
                best = jnp.maximum(best, found[:, :, ROWS:])
            highest[heads] = best if fresh else jnp.maximum(highest[heads], best)
            return carry

        lax.fori_loop(0, HK, body, 0)

    near = NEAR * ROWS

    def soft_near(h, carry):
        top = jnp.max(mx[h], axis=1, keepdims=True)
        raised = jnp.exp2((sc[h, :, :near] - top) * F32(EXP2))
        sc[h, :, :near] = raised
        top1[h] = jnp.broadcast_to(top, (ROWS, ROWS))
        sum1[h] = jnp.broadcast_to(jnp.sum(raised, axis=1, keepdims=True), (ROWS, ROWS))
        return carry

    def soft_far(h, carry):
        top = jnp.max(mx2[h], axis=1, keepdims=True)
        raised = jnp.exp2((sc[h, :, near:] - top) * F32(EXP2))
        sc[h, :, near:] = raised
        total = jnp.sum(raised, axis=1, keepdims=True)
        before = top1[h]
        highest = jnp.maximum(before, top)
        lift1 = jnp.exp2((before - highest) * F32(EXP2))
        lift2 = jnp.exp2((top - highest) * F32(EXP2))
        total = sum1[h] * lift1 + total * lift2
        share = 1.0 / total
        rl[h] = lift1 * share
        rl2[h] = lift2 * share
        value = highest * F32(SCALE) + jnp.log(total)
        stat[...] = jnp.where(lane == h, value, stat[...])
        return carry

    def weighted(step, heads, low, high, factor):
        chosen = pl.ds(step * heads, heads)
        lift = jnp.tile(factor[chosen], (1, 1, high - low))
        weights = (sc[chosen, :, low * ROWS:high * ROWS] * lift).astype(BF16)
        lanes = pl.ds(pl.multiple_of((step * heads // GROUP) * HD, HD), HD)
        rows = vb[low:high, :, lanes].reshape((high - low) * ROWS, HD)
        return lax.dot_general(
            weights.reshape(heads * ROWS, (high - low) * ROWS), rows,
            (((1,), (0,)), ((), ())), preferred_element_type=F32,
        ).reshape(heads, ROWS, HD)

    def weighted_near(step, carry):
        top1[pl.ds(step * NEAR_HEADS, NEAR_HEADS)] = weighted(step, NEAR_HEADS, 0, NEAR, rl)
        return carry

    def weighted_far(step, carry):
        out = weighted(step, FAR_HEADS, NEAR, ROLES, rl2)
        out = (out + top1[pl.ds(step * FAR_HEADS, FAR_HEADS)]).astype(BF16)
        for i in range(FAR_HEADS):
            ctx[0, :, pl.ds(pl.multiple_of((step * FAR_HEADS + i) * HD, HD), HD)] = out[i]
        return carry

    def loop(body, low, high):
        lax.fori_loop(low, high, body, 0, unroll=4)

    pl.semaphore_wait(met, 1)
    for d in range(1, 4):
        pl.semaphore_signal(
            ready, inc=1, device_id=(s, (a + 8 * d) % 32), device_id_type=MESH
        )

    scores(0, 1, mx, True)
    arrive(0, 1)
    send(0, 4, 5)
    arrive(0, 2)
    send(0, 6, 7)

    slots = lax.broadcasted_iota(jnp.int32, (256, 32), 0)
    slot_rank = slots // 64 + 4 * (slots % 2)
    tasks = lax.broadcasted_iota(jnp.int32, (256, 32), 1)
    lengths = tl[pl.ds(a, 1), :]
    workers = ws[pl.ds(a, 1), :]
    picked = workers == slots % 64 // 2
    which = jnp.sum(jnp.where(picked, tasks, 0), axis=1, keepdims=True)
    length = jnp.sum(jnp.where(picked, lengths, 0), axis=1, keepdims=True)
    start = jnp.sum(jnp.where(tasks < which, lengths, 0), axis=1, keepdims=True)
    rank = slot_rank[:, :1]
    token = lax.broadcasted_iota(jnp.int32, (256, ROWS), 1)
    table[...] = jnp.where((token == start + rank) & (rank < length), F32(1), F32(0))
    stat[...] = jnp.zeros_like(stat)

    scores(1, 2, mx, False)
    relay(0)
    arrive(0, 3)
    arrive(0, 4)
    send(0, 8, 9)
    arrive(1, 1)
    send(1, 4, 5)
    scores(3, 2, mx, False)
    relay(1)
    arrive(0, 5)
    arrive(0, 6)
    send(0, 10, 11)
    arrive(1, 2)
    send(1, 6, 7)
    scores(5, 2, mx, False)
    loop(soft_near, 0, 16)
    relay(2)
    arrive(1, 3)
    arrive(1, 4)
    send(1, 8, 9)
    loop(soft_near, 16, HQ)
    arrive(0, 7)
    arrive(0, 8)
    scores(7, 2, mx2, True)
    relay(3)
    arrive(1, 5)
    arrive(1, 6)
    send(1, 10, 11)
    loop(soft_far, 0, HQ)

    pl.semaphore_wait(ready, 3)
    packed = jnp.zeros((64, ROWS), F32)
    for i in range(4):
        moved = stat[...] if i == 0 else pltpu.roll(stat[...], 32 * i, 1)
        packed = packed + lax.dot_general(
            table[i * 64:(i + 1) * 64], moved, (((1,), (0,)), ((), ())),
            precision=lax.Precision.HIGHEST, preferred_element_type=F32,
        )
    pack[...] = packed.reshape(32, 2, ROWS)
    tasks_out = [
        pltpu.make_async_remote_copy(
            pack.at[(a + d) % 32], t2.at[a], s_send.at[d - 1], s_recv.at[d - 1],
            device_id=(s, (a + d) % 32), device_id_type=MESH,
        )
        for d in range(1, 32)
    ]
    for copy in tasks_out:
        copy.start()
    t2[pl.ds(a, 1)] = pack[pl.ds(a, 1)]
    pl.when(held_back)(rest.start)
    relay(4)

    lax.fori_loop(0, HQ // NEAR_HEADS, weighted_near, 0)
    for role in (7, 8):
        arrive(1, role)
    lax.fori_loop(0, HQ // FAR_HEADS, weighted_far, 0)
    for copy in tasks_out:
        copy.wait()
    turned = t2[...].reshape(64, ROWS).T
    turned = jnp.concatenate([turned[32 * i:32 * (i + 1)] for i in range(4)], axis=1)
    source = lax.broadcasted_iota(jnp.int32, (256, 256), 0)
    slot = lax.broadcasted_iota(jnp.int32, (256, 256), 1)
    spread = jnp.where(slot == 4 * (source % 64) + source // 64, F32(1), F32(0))
    lse[0] = lax.dot_general(
        turned, spread, (((1,), (0,)), ((), ())),
        precision=lax.Precision.HIGHEST, preferred_element_type=F32,
    )

    for t in range(2):
        for cond, copy in moves[t]:
            pl.when(cond)(copy.wait_send)
    for i in range(LONG):
        pl.when(own_long > i)(leg1(i).wait_send)
        pl.when(mid_long > i)(leg2(i).wait_send)
        pl.when((s < 7) & (own_long <= i))(piece(i).wait_send)

    @pl.when(s < 7)
    def _():
        main.wait_send()
        rest.wait_send()

    @pl.when(s > 0)
    def _():
        for i in range(LONG):
            piece(i).wait_recv()
        main.wait_recv()
        rest.wait_recv()


def deliver(*refs):
    count = len(refs) // 2
    sems = refs[-1]
    copies = [
        pltpu.make_async_copy(refs[i], refs[count + i], sems.at[i]) for i in range(count)
    ]
    for copy in copies:
        copy.start()
    for copy in copies:
        copy.wait()


def shards(queries, keys, values, handoff, doc_lengths, task_lengths, assignment):
    anywhere = pl.BlockSpec(memory_space=pltpu.HBM)
    local = pl.BlockSpec(memory_space=pltpu.VMEM)
    dma = pltpu.SemaphoreType.DMA
    results = pl.pallas_call(
        kernel,
        out_shape=(
            pltpu.VMEM((1, ROWS, HQ * HD), BF16),
            pltpu.VMEM((1, HQ, 256), F32),
            pltpu.VMEM((1, ROWS, WIDE), BF16),
        ),
        in_specs=[anywhere] * 7,
        out_specs=(local, local, local),
        scratch_shapes=[
            pltpu.VMEM((HQ, ROWS, HD), BF16),
            pltpu.VMEM((ROLES, ROWS, HK * HD), BF16),
            pltpu.VMEM((ROLES, ROWS, HK * HD), BF16),
            pltpu.VMEM((HQ, ROWS, ROLES * ROWS), F32),
            *[pltpu.VMEM((HQ, ROWS, ROWS), F32)] * 6,
            pltpu.VMEM((ROWS, ROWS), F32),
            pltpu.VMEM((256, ROWS), F32),
            pltpu.VMEM((LONG // 2 * PIECE, WIDE), BF16),
            pltpu.SMEM((1, 8), jnp.int32),
            pltpu.VMEM((32, 32), jnp.int32),
            pltpu.VMEM((32, 32), jnp.int32),
            pltpu.VMEM((32, 2, ROWS), F32),
            pltpu.VMEM((32, 2, ROWS), F32),
            dma((HQ,)),
            dma((2,)),
            dma((3,)),
            dma((2, 12)),
            dma((2, ROLES)),
            dma((LONG + 2,)),
            dma((LONG + 2,)),
            dma((2 * LONG,)),
            dma((LONG,)),
            dma((31,)),
            dma((31,)),
            pltpu.SemaphoreType.REGULAR,
            pltpu.SemaphoreType.REGULAR,
        ],
        compiler_params=pltpu.CompilerParams(
            collective_id=0, has_side_effects=True, vmem_limit_bytes=52 << 20
        ),
    )(queries, keys, values, handoff, doc_lengths, task_lengths, assignment)
    context, stats, received = pl.pallas_call(
        deliver,
        out_shape=tuple(jax.ShapeDtypeStruct(r.shape, r.dtype) for r in results),
        in_specs=[local] * 3,
        out_specs=(anywhere,) * 3,
        scratch_shapes=[dma((3,))],
    )(*[pltpu.with_memory_space_constraint(r, pltpu.VMEM) for r in results])
    return context, jnp.swapaxes(stats, 1, 2), received


def solution(mesh):
    rows = P("section", "attn", None)
    small = P("section", None, None)
    return jax.shard_map(
        shards,
        mesh=mesh,
        in_specs=(rows, rows, rows, rows, P("section", None), small, small),
        out_specs=(rows, rows, rows),
        check_vma=False,
    )
```
